128 devices in a mesh: shot: 16 (over y, z), recv: 8 (over x, core).
Axes of the slice: x: 4, y: 4, z: 4, core: 2. Of those that a mesh axis runs over, the one named last changes fastest.
Arguments:
- shot_feats: bfloat16 [64, 64, 256, 384], P(None, 'shot', 'recv'), may hold values from -40 to 40
- norm_gain: float32 [64], replicated, may hold values from 0.25 to 1.75
- shot_taps: float32 [2, 2, 64, 5], replicated, may hold values from -3 to 3
- shot_mix: bfloat16 [2, 64, 64], replicated, may hold values from -0.75 to 0.75
- shot_bias: float32 [2, 64], replicated, may hold values from -0.5 to 0.5
- recv_taps: float32 [2, 2, 64, 5], replicated, may hold values from -3 to 3
- recv_mix: bfloat16 [2, 64, 64], replicated, may hold values from -0.75 to 0.75
- recv_bias: float32 [2, 64], replicated, may hold values from -0.5 to 0.5
- pack_index: int32 [2048, 12], P(('shot', 'recv')), may hold values from -1 to 127, as said below
- recv_index: int32 [1024, 24], P(('shot', 'recv')), may hold values from -1 to 191, as said below
Outputs:
- recv_feats: bfloat16 [64, 1024, 24, 384], P(None, ('shot', 'recv'))
The draws below stay inside these ranges and needn't reach their ends.
Inputs may be any that keep to these rules, and one draw needn't show every extreme that they name: `pack_index`: on each device's 16 rows every local trace (local shot * 32 + trace within the tile) is named exactly once; live slots of a row come first, the rest are -1; on every device some row has all 12 slots live. `recv_index`: within receiver block d of tile j every live slot c of row d of the pack_index rows of each shot block s of tile j is named exactly once, as s * 12 + c, and nothing else is named; a receiver's live slots come first and are ordered by shot, then trace; each receiver has from 8 to 24 live slots, and every block has a receiver with all 24 live.
All inputs are finite; a program needn't handle non-finite values.
Results may differ from the reference program's by a relative error of at most 0.015.
Values may be sent and summed in bfloat16 or wider, within the bound.
No kernel may reach another device: no remote copies, remote signals or barrier semaphores. Data moves between devices by JAX's collectives and lax.ppermute only.
A program may use at most 128 MiB of HBM per device.

```python
import jax
import jax.numpy as jnp
from jax import lax

C = 64
NT = 384
SHOT_DEV = 4
TRACES = 256
LAYERS = 2
RCV_DEV = 8
NBLK = 16
NTILE = 8
SHOTS = 64
TILE_TR = 32
CAP = 12
FOLD = 24
RECVS = 1024


def geometry(key):
    live_count = SHOT_DEV * TILE_TR
    mean_send = live_count // NBLK
    mean_fold = live_count // RCV_DEV
    entries = NBLK * CAP

    def one_tile(tile_key):
        keys = jax.random.split(tile_key, 6)
        spread_half = jax.random.randint(keys[0], (NBLK // 2,), 0, mean_send // 2 + 1)
        spread_half = spread_half.at[0].set(mean_send // 2)
        counts = jnp.concatenate([mean_send + spread_half, mean_send - spread_half])
        counts = counts[jax.random.permutation(keys[1], NBLK)]
        rotate = (jnp.arange(NBLK)[None, :] - jnp.arange(NBLK)[:, None]) % NBLK
        sends = counts[rotate]
        starts = jnp.cumsum(sends, axis=1) - sends
        orders = jax.vmap(lambda sub_key: jax.random.permutation(sub_key, live_count))(jax.random.split(keys[2], NBLK))
        slot_ids = jnp.arange(CAP)
        where_at = jnp.clip(starts[:, :, None] + slot_ids[None, None, :], 0, live_count - 1)
        filled = slot_ids[None, None, :] < sends[:, :, None]
        source_rows = jnp.broadcast_to(jnp.arange(NBLK)[:, None, None], where_at.shape)
        packed = jnp.where(filled, orders[source_rows, where_at], -1).astype(jnp.int32)
        fold_half = jax.random.randint(keys[3], (NBLK, RCV_DEV // 2), 0, mean_fold // 2 + 1)
        fold_half = fold_half.at[:, 0].set(mean_fold // 2)
        folds = jnp.concatenate([mean_fold + fold_half, mean_fold - fold_half], axis=1)
        shuffles = jax.vmap(lambda sub_key: jax.random.permutation(sub_key, RCV_DEV))(jax.random.split(keys[5], NBLK))
        folds = jnp.take_along_axis(folds, shuffles, axis=1)

        def one_target(target, fold_counts, target_key):
            column = lax_index(packed, target).reshape(entries)
            valid = column >= 0
            priority = jax.random.permutation(target_key, entries)
            score = jnp.where(valid, priority, priority + entries)
            arrival = jnp.argsort(score)[:live_count]
            ends = jnp.cumsum(fold_counts)
            ranks = jnp.arange(live_count)
            receiver = jnp.sum(ranks[:, None] >= ends[None, :], axis=1)
            local = column[arrival]
            source_block = arrival // CAP
            shot_index = source_block * SHOT_DEV + local // TILE_TR
            sort_key = receiver * (SHOTS * TILE_TR) + shot_index * TILE_TR + local % TILE_TR
            ordered = jnp.argsort(sort_key)
            receiver_sorted = receiver[ordered]
            begins = ends - fold_counts
            slot_pos = ranks - begins[receiver_sorted]
            empty_table = jnp.full((RCV_DEV, FOLD), -1, jnp.int32)
            return empty_table.at[receiver_sorted, slot_pos].set(arrival[ordered].astype(jnp.int32))
        unpacked = jax.vmap(one_target)(jnp.arange(NBLK), folds, jax.random.split(keys[4], NBLK))
        return (packed, unpacked)
    packed, unpacked = jax.vmap(one_tile)(jax.random.split(key, NTILE))
    pack_rows = jnp.transpose(packed, (1, 0, 2, 3)).reshape(NBLK * NTILE * NBLK, CAP)
    recv_rows = jnp.transpose(unpacked, (1, 0, 2, 3)).reshape(RECVS, FOLD)
    return (pack_rows.astype(jnp.int32), recv_rows.astype(jnp.int32))


def lax_index(packed, target):
    return jnp.take(packed, target, axis=1)


def draw_pack_index(key, part):
    return geometry(key)[0]


def draw_recv_index(key, part):
    return geometry(key)[1]


def draw_shot_feats(key, part):
    key = jax.random.fold_in(key, 7)
    keys = jax.random.split(key, 3)
    full_shape = (C, SHOTS, TRACES, NT)
    decay = 10.0 ** (-jnp.arange(TRACES, dtype=jnp.float32) / (TRACES - 1))
    shot_scale = jnp.exp(jax.random.uniform(keys[0], (SHOTS,), jnp.float32, jnp.log(0.3), jnp.log(3.0)))
    channel_scale = jnp.exp(jax.random.uniform(keys[1], (C,), jnp.float32, jnp.log(0.5), jnp.log(2.0)))
    base = jnp.clip(jax.random.normal(keys[2], full_shape, jnp.float32), -6.0, 6.0)
    values = base * channel_scale[:, None, None, None] * shot_scale[None, :, None, None] * decay[None, None, :, None]
    return jnp.clip(values, -40.0, 40.0).astype(jnp.bfloat16)


def normal_values(key, dims, deviation, reach, held_as=jnp.bfloat16):
    drawn = jax.random.normal(key, dims, jnp.float32) * deviation
    return jnp.minimum(jnp.maximum(drawn, -reach), reach).astype(held_as)


def setup_inputs(seed: int = 0) -> dict:
    seeds = jax.random.split(jax.random.key(seed), 11)
    shot_feats = draw_shot_feats(jax.random.fold_in(seeds[10], 71), 0)
    norm_gain = jnp.clip(1.0 + 0.15 * jax.random.normal(seeds[1], (C,), jnp.float32), 0.25, 1.75)
    shot_taps = normal_values(seeds[2], (LAYERS, 2, C, 5), 0.5, 3.0, jnp.float32)
    shot_mix = normal_values(seeds[3], (LAYERS, C, C), C ** -0.5, 0.75)
    shot_bias = jnp.clip(jax.random.uniform(seeds[4], (LAYERS, C), jnp.float32, -0.5, 0.5), -0.5, 0.5)
    recv_taps = normal_values(seeds[5], (LAYERS, 2, C, 5), 0.5, 3.0, jnp.float32)
    recv_mix = normal_values(seeds[6], (LAYERS, C, C), C ** -0.5, 0.75)
    recv_bias = jnp.clip(jax.random.uniform(seeds[7], (LAYERS, C), jnp.float32, -0.5, 0.5), -0.5, 0.5)
    pack_index = draw_pack_index(jax.random.fold_in(seeds[10], 71), 0)
    recv_index = draw_recv_index(jax.random.fold_in(seeds[10], 71), 0)
    return dict(shot_feats=shot_feats, norm_gain=norm_gain, shot_taps=shot_taps, shot_mix=shot_mix, shot_bias=shot_bias, recv_taps=recv_taps, recv_mix=recv_mix, recv_bias=recv_bias, pack_index=pack_index, recv_index=recv_index)


def dilated(padded, kernel, axis_index, length):
    target = (kernel.shape[0],) + (1,) * (padded.ndim - 1)
    summed = kernel[:, 0].reshape(target) * lax.slice_in_dim(padded, 0, length, axis=axis_index)
    for offset in range(1, 5):
        summed = summed + kernel[:, offset].reshape(target) * lax.slice_in_dim(padded, 2 * offset, 2 * offset + length, axis=axis_index)
    return summed

def zero_conv(values, kernel, axis_index):
    widths = [(0, 0)] * values.ndim
    widths[axis_index] = (4, 4)
    return dilated(jnp.pad(values, widths), kernel, axis_index, values.shape[axis_index])

def mixing(inputs, weight, bias_row):
    product = jnp.einsum('oc,cabd->oabd', weight.astype(jnp.float32), inputs.astype(jnp.float32))
    return jax.nn.relu(product + bias_row[:, None, None, None])

def reference(shot_feats, norm_gain, shot_taps, shot_mix, shot_bias, recv_taps, recv_mix, recv_bias, pack_index, recv_index):
    margin = 4 * LAYERS
    energy = lax.optimization_barrier(jnp.sum(jnp.square(shot_feats.astype(jnp.float32)), axis=(0, 2, 3)))
    shot_rms = jnp.sqrt(energy / (C * TRACES * NT) + 1e-05)
    scaled_by = norm_gain[:, None, None, None] / shot_rms[None, :, None, None]
    extended = jnp.pad(shot_feats, ((0, 0), (0, 0), (margin, margin), (0, 0)))
    pack_four = pack_index.reshape(NBLK, NTILE, NBLK, CAP)
    recv_four = recv_index.reshape(NBLK, NTILE, RCV_DEV, FOLD)

    def one_tile(tile_index):
        span = TILE_TR + 2 * margin
        window = lax.dynamic_slice_in_dim(extended, (tile_index * TILE_TR).astype(jnp.int32), span, axis=2)
        positions = tile_index * TILE_TR - margin + jnp.arange(span, dtype=jnp.int32)
        inside = ((positions >= 0) & (positions < TRACES)).astype(jnp.float32)[None, None, :, None]
        current = window.astype(jnp.float32) * scaled_by
        for depth in range(LAYERS):
            across = zero_conv(current, shot_taps[depth, 0], 2)
            mixed_in = zero_conv(across, shot_taps[depth, 1], 3).astype(jnp.bfloat16)
            current = (mixing(mixed_in, shot_mix[depth], shot_bias[depth]) * inside).astype(jnp.bfloat16)
        central = current[:, :, margin:margin + TILE_TR, :]
        slot_table = lax.dynamic_index_in_dim(recv_four, tile_index, axis=1, keepdims=False)
        pack_table = lax.dynamic_index_in_dim(pack_four, tile_index, axis=1, keepdims=False)
        live_slot = slot_table >= 0
        clipped = jnp.maximum(slot_table, 0).astype(jnp.int32)
        source_block = clipped // CAP
        source_slot = clipped % CAP
        target_block = jnp.broadcast_to(jnp.arange(NBLK, dtype=jnp.int32)[:, None, None], clipped.shape)
        local_trace = jnp.maximum(pack_table[source_block, target_block, source_slot], 0).astype(jnp.int32)
        shot_index = source_block * SHOT_DEV + local_trace // TILE_TR
        flat_index = jnp.clip(shot_index * TILE_TR + local_trace % TILE_TR, 0, SHOTS * TILE_TR - 1).astype(jnp.int32)
        flat_feats = central.reshape(C, SHOTS * TILE_TR, NT)
        gathered = jnp.take(flat_feats, flat_index.reshape(-1), axis=1)
        regrouped = jnp.where(live_slot.reshape(1, -1, 1), gathered, jnp.zeros((), gathered.dtype))
        regrouped = regrouped.reshape(C, NBLK * RCV_DEV, FOLD, NT)
        live_mask = live_slot.reshape(NBLK * RCV_DEV, FOLD).astype(jnp.float32)[None, :, :, None]
        for depth in range(LAYERS):
            across = zero_conv(regrouped, recv_taps[depth, 0], 2)
            mixed_in = zero_conv(across, recv_taps[depth, 1], 3).astype(jnp.bfloat16)
            regrouped = (mixing(mixed_in, recv_mix[depth], recv_bias[depth]) * live_mask).astype(jnp.bfloat16)
        return regrouped.reshape(C, NBLK, RCV_DEV, FOLD, NT)
    stacked = lax.map(one_tile, jnp.arange(NTILE, dtype=jnp.int32))
    return jnp.transpose(stacked, (1, 2, 0, 3, 4, 5)).reshape(C, RECVS, FOLD, NT)
```

```python
import functools

import jax
import jax.numpy as jnp
from jax import lax
from jax.experimental import pallas as pl
from jax.experimental.pallas import tpu as pltpu
from jax.sharding import PartitionSpec as P

TRACES = 256
LAYERS = 2
HALO = 8
GROUP = 8
LANES = 128
BF16 = jnp.bfloat16
F32 = jnp.float32


def lagged(values, lag):
    if lag == 0:
        return values
    samples = values.shape[1]
    turned = pltpu.roll(values, (-lag) % samples, 1)
    lane = lax.broadcasted_iota(jnp.int32, values.shape, 1)
    inside = lane < samples - lag if lag > 0 else lane >= -lag
    return jnp.where(inside, turned, jnp.zeros((), values.dtype))


def group_linear(source, first, taps, weight, count):
    channels, samples = source.shape[1:]
    part = 16
    tiles = samples // LANES
    filtered = [[[None] * tiles for _ in range(channels // part)] for _ in range(count)]
    for h in range(channels // part):
        rows_at = slice(h * part, (h + 1) * part)
        for j in range(tiles):
            lanes_at = slice(j * LANES, (j + 1) * LANES)
            tap = [taps[k, rows_at, :] for k in range(5)]
            rows = [source[first + i, rows_at, lanes_at].astype(F32) for i in range(count + 8)]
            for q in range(count):
                term = [rows[q + 2 * k] * tap[k] for k in range(5)]
                total = ((term[0] + term[1]) + (term[2] + term[3])) + term[4]
                filtered[q][h][j] = total.astype(BF16)
    outs = []
    for q in range(count):
        across = jnp.concatenate(
            [jnp.concatenate(pieces, axis=1) for pieces in filtered[q]], axis=0
        )
        stacked = jnp.concatenate([lagged(across, 2 * k - 4) for k in range(5)], axis=0)
        outs.append(jnp.dot(weight[...], stacked, preferred_element_type=F32))
    return outs


def shot_kernel(
    inverse_rms,
    slot_of,
    edges,
    main,
    low,
    high,
    taps,
    weights,
    bias,
    packed,
    turned,
    grid_in,
    first_out,
    last_out,
    sems,
):
    shot = pl.program_id(0)
    shots = pl.num_programs(0)
    channels, _, here, samples = main.shape
    span = here + 2 * HALO
    tiles = samples // LANES

    def load_channel(i, _):
        for q in range(2):
            c = i * 2 + q
            base = pl.multiple_of(c * span, 8)
            for j in range(tiles):
                at = slice(j * LANES, (j + 1) * LANES)
                turned[j, pl.ds(base, HALO), :] = low[c, 0, :, at].astype(F32)
                turned[j, pl.ds(base + HALO, here), :] = main[c, 0, :, at].astype(F32)
                turned[j, pl.ds(base + HALO + here, HALO), :] = high[c, 0, :, at].astype(F32)
        return 0

    lax.fori_loop(0, channels // 2, load_channel, 0)

    def gather_trace(i, _):
        for q in range(4):
            t = i * 4 + q
            for j in range(tiles):
                at = slice(j * LANES, (j + 1) * LANES)
                grid_in[t, :, at] = turned[j, pl.ds(t, channels, stride=span), :].astype(BF16)
        return 0

    lax.fori_loop(0, span // 4, gather_trace, 0)

    scale = inverse_rms[shot]
    count = here + 8

    def first_layer(i, _):
        outs = group_linear(grid_in, i * GROUP, taps.at[0], weights.at[0], GROUP)
        for q in range(GROUP):
            t = i * GROUP + q
            value = jnp.maximum(outs[q] * scale + bias[0], 0.0)
            first_out[t] = value.astype(BF16)
        return 0

    lax.fori_loop(0, count // GROUP, first_layer, 0)

    @pl.when(edges[0] == 1)
    def _():
        first_out[0:4] = jnp.zeros((4, channels, samples), BF16)

    @pl.when(edges[1] == 1)
    def _():
        first_out[here + 4 : here + 8] = jnp.zeros((4, channels, samples), BF16)

    half = lax.rem(shot, 2)

    def drain(which):
        pltpu.make_async_copy(
            last_out.at[which], packed.at[pl.ds(0, here)], sems.at[which]
        ).wait()

    @pl.when(shot >= 2)
    def _():
        drain(half)

    def second_layer(i, _):
        outs = group_linear(first_out, i * GROUP, taps.at[1], weights.at[1], GROUP)
        for q in range(GROUP):
            t = i * GROUP + q
            value = jnp.maximum(outs[q] + bias[1], 0.0)
            last_out[half, t] = value.astype(BF16)
        for q in range(GROUP):
            t = i * GROUP + q
            pltpu.make_async_copy(
                last_out.at[half, t], packed.at[slot_of[shot * here + t]], sems.at[half]
            ).start()
        return 0

    lax.fori_loop(0, here // GROUP, second_layer, 0)

    @pl.when(shot == shots - 1)
    def _():
        drain(1 - half)
        drain(half)


def recv_kernel(
    keep,
    live_count,
    buffer,
    taps,
    weights,
    bias,
    out,
    gathered,
    middle,
    turned,
    sems,
):
    row = pl.program_id(0)
    rows = pl.num_programs(0)
    channels, _, fold, samples = out.shape
    tiles = samples // LANES
    half = lax.rem(row, 2)

    def fetch(r, into):
        def one(k, _):
            pltpu.make_async_copy(
                buffer.at[keep[r * fold + k]], gathered.at[into, 4 + k], sems.at[into]
            ).start()
            return 0

        lax.fori_loop(0, fold, one, 0)

    @pl.when(row == 0)
    def _():
        fetch(0, 0)
        edge = jnp.zeros((4, channels, samples), BF16)
        for which in range(2):
            gathered[which, 0:4] = edge
            gathered[which, fold + 4 : fold + 8] = edge
        middle[0:4] = edge
        middle[fold + 4 : fold + 8] = edge

    @pl.when(row + 1 < rows)
    def _():
        fetch(row + 1, 1 - half)

    pltpu.make_async_copy(
        buffer.at[pl.ds(0, fold)], gathered.at[half, pl.ds(4, fold)], sems.at[half]
    ).wait()
    live = live_count[row]

    def clear(k, _):
        gathered[half, 4 + k] = jnp.zeros((channels, samples), BF16)
        return 0

    lax.fori_loop(live, fold, clear, 0)
    groups = (live + GROUP - 1) // GROUP

    def first_layer(i, _):
        outs = group_linear(gathered.at[half], i * GROUP, taps.at[0], weights.at[0], GROUP)
        for q in range(GROUP):
            k = i * GROUP + q
            value = jnp.maximum(outs[q] + bias[0], 0.0)
            middle[4 + k] = jnp.where(k < live, value, 0.0).astype(BF16)
        return 0

    lax.fori_loop(0, groups, first_layer, 0)

    def clear_rest(k, _):
        middle[4 + k] = jnp.zeros((channels, samples), BF16)
        for j in range(tiles):
            turned[j, pl.ds(k, channels, stride=fold), :] = jnp.zeros((channels, LANES), F32)
        return 0

    lax.fori_loop(groups * GROUP, fold, clear_rest, 0)

    def second_layer(i, _):
        outs = group_linear(middle, i * GROUP, taps.at[1], weights.at[1], GROUP)
        for q in range(GROUP):
            k = i * GROUP + q
            value = jnp.where(k < live, jnp.maximum(outs[q] + bias[1], 0.0), 0.0)
            for j in range(tiles):
                turned[j, pl.ds(k, channels, stride=fold), :] = value[:, j * LANES : (j + 1) * LANES]
        return 0

    lax.fori_loop(0, groups, second_layer, 0)

    def store_channel(i, _):
        for q in range(4):
            c = i * 4 + q
            base = pl.multiple_of(c * fold, 8)
            for j in range(tiles):
                out[c, 0, :, j * LANES : (j + 1) * LANES] = turned[j, pl.ds(base, fold), :].astype(BF16)
        return 0

    lax.fori_loop(0, channels // 4, store_channel, 0)


def whole(*shape):
    return pl.BlockSpec(shape, lambda *_: (0,) * len(shape))


def tap_tables(taps):
    table = jnp.swapaxes(taps[:, 0], 1, 2)[..., None]
    return jnp.broadcast_to(table, table.shape[:-1] + (LANES,)).astype(F32)


def mix_tables(mix, taps, gain):
    layers, outs, channels = mix.shape
    product = mix.astype(F32)[:, :, None, :] * jnp.swapaxes(taps[:, 1], 1, 2)[:, None, :, :]
    if gain is not None:
        product = product * gain
    return product.reshape(layers, outs, 5 * channels).astype(BF16)


def per_device(
    shot_feats,
    norm_gain,
    shot_taps,
    shot_mix,
    shot_bias,
    recv_taps,
    recv_mix,
    recv_bias,
    pack_index,
    recv_index,
):
    channels, shots_here, here, samples = shot_feats.shape
    blocks, capacity = pack_index.shape
    rows_here, fold = recv_index.shape
    slots = blocks * capacity
    span = here + 2 * HALO

    tiles_all = lax.axis_size("recv")
    tile = lax.axis_index("recv")
    forward = [(i, i + 1) for i in range(tiles_all - 1)]
    backward = [(i + 1, i) for i in range(tiles_all - 1)]
    low = lax.ppermute(shot_feats[:, :, here - HALO :, :], "recv", forward)
    high = lax.ppermute(shot_feats[:, :, :HALO, :], "recv", backward)
    energy = lax.psum(jnp.sum(jnp.square(shot_feats.astype(F32)), axis=(0, 2, 3)), "recv")
    inverse_rms = 1.0 / jnp.sqrt(energy / (channels * TRACES * samples) + 1e-05)

    packs = pack_index.reshape(-1)
    trace_id = jnp.arange(shots_here * here, dtype=jnp.int32)
    slot_id = jnp.arange(slots, dtype=jnp.int32)
    slot_of = jnp.sum(
        jnp.where(packs[None, :] == trace_id[:, None], slot_id[None, :], 0), axis=1
    ).astype(jnp.int32)
    edges = jnp.stack([tile == 0, tile == tiles_all - 1]).astype(jnp.int32)

    gain_rows = jnp.stack([norm_gain] + [jnp.ones_like(norm_gain)] * (LAYERS - 1))
    weights = mix_tables(shot_mix, shot_taps, gain_rows[:, None, None, :])
    bias = jnp.broadcast_to(shot_bias[:, :, None], shot_bias.shape + (samples,))
    smem = pl.BlockSpec(memory_space=pltpu.SMEM)
    packed = pl.pallas_call(
        shot_kernel,
        grid=(shots_here,),
        in_specs=[
            smem,
            smem,
            smem,
            pl.BlockSpec((channels, 1, here, samples), lambda s: (0, s, 0, 0)),
            pl.BlockSpec((channels, 1, HALO, samples), lambda s: (0, s, 0, 0)),
            pl.BlockSpec((channels, 1, HALO, samples), lambda s: (0, s, 0, 0)),
            whole(LAYERS, 5, channels, LANES),
            whole(LAYERS, channels, 5 * channels),
            whole(LAYERS, channels, samples),
        ],
        out_specs=pl.BlockSpec(memory_space=pl.ANY),
        out_shape=jax.ShapeDtypeStruct((slots, channels, samples), BF16),
        scratch_shapes=[
            pltpu.VMEM((samples // LANES, channels * span, LANES), F32),
            pltpu.VMEM((span, channels, samples), BF16),
            pltpu.VMEM((here + 8, channels, samples), BF16),
            pltpu.VMEM((2, here, channels, samples), BF16),
            pltpu.SemaphoreType.DMA((2,)),
        ],
        compiler_params=pltpu.CompilerParams(vmem_limit_bytes=48 * 2**20),
        name="shot_domain",
    )(inverse_rms, slot_of, edges, shot_feats, low, high, tap_tables(shot_taps), weights, bias)

    buffer = lax.all_to_all(
        packed.reshape(blocks, capacity, channels, samples),
        "shot",
        split_axis=0,
        concat_axis=0,
        tiled=True,
    ).reshape(slots, channels, samples)

    keep = jnp.maximum(recv_index.reshape(-1), 0)
    live_count = jnp.sum(recv_index >= 0, axis=1).astype(jnp.int32)
    recv_bias_rows = jnp.broadcast_to(recv_bias[:, :, None], recv_bias.shape + (samples,))
    return pl.pallas_call(
        recv_kernel,
        grid=(rows_here,),
        in_specs=[
            smem,
            smem,
            pl.BlockSpec(memory_space=pl.ANY),
            whole(LAYERS, 5, channels, LANES),
            whole(LAYERS, channels, 5 * channels),
            whole(LAYERS, channels, samples),
        ],
        out_specs=pl.BlockSpec((channels, 1, fold, samples), lambda r: (0, r, 0, 0)),
        out_shape=jax.ShapeDtypeStruct((channels, rows_here, fold, samples), BF16),
        scratch_shapes=[
            pltpu.VMEM((2, fold + 8, channels, samples), BF16),
            pltpu.VMEM((fold + 8, channels, samples), BF16),
            pltpu.VMEM((samples // LANES, channels * fold, LANES), F32),
            pltpu.SemaphoreType.DMA((2,)),
        ],
        compiler_params=pltpu.CompilerParams(vmem_limit_bytes=48 * 2**20),
        name="recv_domain",
    )(
        keep,
        live_count,
        buffer,
        tap_tables(recv_taps),
        mix_tables(recv_mix, recv_taps, None),
        recv_bias_rows,
    )


def solution(mesh):
    return jax.shard_map(
        per_device,
        mesh=mesh,
        in_specs=(
            P(None, "shot", "recv", None),
            P(),
            P(),
            P(),
            P(),
            P(),
            P(),
            P(),
            P(("shot", "recv"), None),
            P(("shot", "recv"), None),
        ),
        out_specs=P(None, ("shot", "recv"), None, None),
        check_vma=False,
    )
```

```python
import jax
import jax.numpy as jnp
from jax import lax
from jax.experimental import pallas as pl
from jax.experimental.pallas import tpu as pltpu
from jax.sharding import PartitionSpec as P

TRACES = 256
LAYERS = 2
HALO = 8
GROUP = 8
CHUNKS = 3
PITCH = 33
FOLDP = 25
LANES = 128
BF16 = jnp.bfloat16
F32 = jnp.float32


def lagged(values, lag):
    if lag == 0:
        return values
    samples = values.shape[1]
    turned = pltpu.roll(values, (-lag) % samples, 1)
    lane = lax.broadcasted_iota(jnp.int32, values.shape, 1)
    inside = lane < samples - lag if lag > 0 else lane >= -lag
    return jnp.where(inside, turned, jnp.zeros((), values.dtype))


def group_linear(source, first, taps, weight, count):
    split = len(source.shape) == 4
    channels = source.shape[-2]
    part = 16
    tiles = source.shape[0] if split else source.shape[2] // LANES
    filtered = [[[None] * tiles for _ in range(channels // part)] for _ in range(count)]
    for h in range(channels // part):
        rows_at = slice(h * part, (h + 1) * part)
        for j in range(tiles):
            lanes_at = slice(j * LANES, (j + 1) * LANES)
            tap = [taps[k, rows_at, :] for k in range(5)]
            rows = [
                (
                    source[j, first + i, rows_at, :]
                    if split
                    else source[first + i, rows_at, lanes_at]
                ).astype(F32)
                for i in range(count + 8)
            ]
            for q in range(count):
                term = [rows[q + 2 * k] * tap[k] for k in range(5)]
                total = ((term[0] + term[1]) + (term[2] + term[3])) + term[4]
                filtered[q][h][j] = total.astype(BF16)
    outs = []
    for q in range(count):
        across = jnp.concatenate(
            [jnp.concatenate(pieces, axis=1) for pieces in filtered[q]], axis=0
        )
        stacked = jnp.concatenate([lagged(across, 2 * k - 4) for k in range(5)], axis=0)
        outs.append(jnp.dot(weight[...], stacked, preferred_element_type=F32))
    return outs


def last_layer(source, first, trace, base, send, packed, tables, staged, half, sems, at):
    taps, weights, bias = tables
    outs = group_linear(source, first, taps.at[1], weights.at[1], GROUP)
    for q in range(GROUP):
        value = jnp.maximum(outs[q] + bias[1], 0.0).astype(BF16)
        for j in range(CHUNKS):
            staged[half, j, at + q] = value[:, j * LANES : (j + 1) * LANES]
    for q in range(GROUP):
        slot = send[base + trace + q]
        for j in range(CHUNKS):
            pltpu.make_async_copy(
                staged.at[half, j, at + q], packed[j].at[slot], sems.at[half]
            ).start()


def drain(staged, packed, sems, half):
    for j in range(CHUNKS):
        pltpu.make_async_copy(
            staged.at[half, j], packed[j].at[pl.ds(0, staged.shape[2])], sems.at[half]
        ).wait()


def regroup(turned, grid_in, channels):
    span = grid_in.shape[0]

    def gather_trace(i, _):
        for q in range(8):
            t = i * 8 + q
            for j in range(turned.shape[0]):
                at = slice(j * LANES, (j + 1) * LANES)
                grid_in[t, :, at] = turned[j, pl.ds(t, channels, stride=PITCH), :].astype(BF16)
        return 0

    lax.fori_loop(0, span // 8, gather_trace, 0)


def inner_kernel(inverse_rms, send, main, taps, weights, bias, middle, *rest):
    packed, (turned, grid_in, staged, sems) = rest[:CHUNKS], rest[CHUNKS:]
    shot = pl.program_id(0)
    channels, _, here, samples = main.shape
    half = lax.rem(shot, 2)

    def load_channel(i, _):
        for q in range(4):
            c = i * 4 + q
            base = c * PITCH
            for j in range(turned.shape[0]):
                at = slice(j * LANES, (j + 1) * LANES)
                turned[j, pl.ds(base, here), :] = main[c, 0, :, at].astype(F32)
        return 0

    lax.fori_loop(0, channels // 4, load_channel, 0)
    regroup(turned, grid_in, channels)
    scale = inverse_rms[shot]

    def first_layer(i, _):
        outs = group_linear(grid_in, i * GROUP, taps.at[0], weights.at[0], GROUP)
        for q in range(GROUP):
            value = jnp.maximum(outs[q] * scale + bias[0], 0.0)
            middle[0, i * GROUP + q] = value.astype(BF16)
        return 0

    lax.fori_loop(0, (here - 8) // GROUP, first_layer, 0)

    @pl.when(shot >= 2)
    def _():
        drain(staged, packed, sems, half)

    def second_layer(i, _):
        last_layer(
            middle.at[0],
            i * GROUP,
            8 + i * GROUP,
            shot * here,
            send,
            packed,
            (taps, weights, bias),
            staged,
            half,
            sems,
            i * GROUP,
        )
        return 0

    lax.fori_loop(0, (here - 16) // GROUP, second_layer, 0)

    @pl.when(shot == pl.num_programs(0) - 1)
    def _():
        drain(staged, packed, sems, 1 - half)
        drain(staged, packed, sems, half)


def edge_kernel(inverse_rms, send, edges, main, low, high, middle, taps, weights, bias, *rest):
    rest = rest[CHUNKS:]
    packed, (turned, grid_in, joined, staged, sems) = rest[:CHUNKS], rest[CHUNKS:]
    shot = pl.program_id(0)
    channels, _, here, samples = main.shape
    span = 4 * HALO
    half = lax.rem(shot, 2)

    def load_channel(i, _):
        for q in range(4):
            c = i * 4 + q
            base = c * PITCH
            for j in range(turned.shape[0]):
                at = slice(j * LANES, (j + 1) * LANES)
                turned[j, pl.ds(base, HALO), :] = low[c, 0, :, at].astype(F32)
                turned[j, pl.ds(base + HALO, HALO), :] = main[c, 0, 0:16, at].astype(F32)[:HALO]
                turned[j, pl.ds(base + 2 * HALO, HALO), :] = main[
                    c, 0, here - 16 : here, at
                ].astype(F32)[16 - HALO :]
                turned[j, pl.ds(base + 3 * HALO, HALO), :] = high[c, 0, :, at].astype(F32)
        return 0

    lax.fori_loop(0, channels // 4, load_channel, 0)
    regroup(turned, grid_in, channels)
    scale = inverse_rms[shot]

    @pl.when(shot >= 2)
    def _():
        drain(staged, packed, sems, half)

    def one_side(side, _):
        outs = group_linear(grid_in, side * 16, taps.at[0], weights.at[0], GROUP)
        for q in range(GROUP):
            value = jnp.maximum(outs[q] * scale + bias[0], 0.0)
            joined[side, side * 8 + q] = value.astype(BF16)
            joined[side, 8 - side * 8 + q] = middle[0, side * 16 + q]

        @pl.when(edges[side] == 1)
        def _():
            joined[side, pl.ds(side * 12, 4)] = jnp.zeros((4, channels, samples), BF16)

        last_layer(
            joined.at[side],
            0,
            side * (here - 8),
            shot * here,
            send,
            packed,
            (taps, weights, bias),
            staged,
            half,
            sems,
            side * GROUP,
        )
        return 0

    lax.fori_loop(0, 2, one_side, 0)

    @pl.when(shot == pl.num_programs(0) - 1)
    def _():
        drain(staged, packed, sems, 1 - half)
        drain(staged, packed, sems, half)


def recv_kernel(
    keep,
    live_count,
    taps,
    weights,
    bias,
    *rest,
):
    buffers, (out, gathered, middle, turned, sems) = rest[:CHUNKS], rest[CHUNKS:]
    row = pl.program_id(0)
    rows = pl.num_programs(0)
    channels, _, fold, samples = out.shape
    tiles = samples // LANES
    half = lax.rem(row, 2)

    def fetch(r, into):
        def one(i, _):
            for q in range(4):
                k = i * 4 + q
                slot = keep[r * fold + k]
                for j in range(CHUNKS):
                    pltpu.make_async_copy(
                        buffers[j].at[slot], gathered.at[into, j, 4 + k], sems.at[into]
                    ).start()
            return 0

        lax.fori_loop(0, fold // 4, one, 0)

    @pl.when(row == 0)
    def _():
        fetch(0, 0)
        edge = jnp.zeros((4, channels, samples), BF16)
        for which in range(2):
            for j in range(CHUNKS):
                gathered[which, j, 0:4] = edge[:, :, :LANES]
                gathered[which, j, fold + 4 : fold + 8] = edge[:, :, :LANES]
        middle[0:4] = edge
        middle[fold + 4 : fold + 8] = edge

    @pl.when(row + 1 < rows)
    def _():
        fetch(row + 1, 1 - half)

    for j in range(CHUNKS):
        pltpu.make_async_copy(
            buffers[j].at[pl.ds(0, fold)], gathered.at[half, j, pl.ds(4, fold)], sems.at[half]
        ).wait()
    live = live_count[row]

    def clear(k, _):
        for j in range(CHUNKS):
            gathered[half, j, 4 + k] = jnp.zeros((channels, LANES), BF16)
        return 0

    lax.fori_loop(live, fold, clear, 0)
    groups = (live + GROUP - 1) // GROUP

    def first_layer(i, _):
        outs = group_linear(gathered.at[half], i * GROUP, taps.at[0], weights.at[0], GROUP)
        for q in range(GROUP):
            k = i * GROUP + q
            value = jnp.maximum(outs[q] + bias[0], 0.0)
            middle[4 + k] = jnp.where(k < live, value, 0.0).astype(BF16)
        return 0

    lax.fori_loop(0, groups, first_layer, 0)

    def clear_rest(k, _):
        middle[4 + k] = jnp.zeros((channels, samples), BF16)
        for j in range(tiles):
            turned[j, pl.ds(k, channels, stride=FOLDP), :] = jnp.zeros((channels, LANES), F32)
        return 0

    lax.fori_loop(groups * GROUP, fold, clear_rest, 0)

    def second_layer(i, _):
        outs = group_linear(middle, i * GROUP, taps.at[1], weights.at[1], GROUP)
        for q in range(GROUP):
            k = i * GROUP + q
            value = jnp.where(k < live, jnp.maximum(outs[q] + bias[1], 0.0), 0.0)
            for j in range(tiles):
                turned[j, pl.ds(k, channels, stride=FOLDP), :] = value[:, j * LANES : (j + 1) * LANES]
        return 0

    lax.fori_loop(0, groups, second_layer, 0)

    def store_channel(i, _):
        for q in range(4):
            c = i * 4 + q
            base = c * FOLDP
            for j in range(tiles):
                out[c, 0, :, j * LANES : (j + 1) * LANES] = turned[j, pl.ds(base, fold), :].astype(BF16)
        return 0

    lax.fori_loop(0, channels // 4, store_channel, 0)


def whole(*shape):
    return pl.BlockSpec(shape, lambda *_: (0,) * len(shape))


def tap_tables(taps):
    table = jnp.swapaxes(taps[:, 0], 1, 2)[..., None]
    return jnp.broadcast_to(table, table.shape[:-1] + (LANES,)).astype(F32)


def mix_tables(mix, taps, gain):
    layers, outs, channels = mix.shape
    product = mix.astype(F32)[:, :, None, :] * jnp.swapaxes(taps[:, 1], 1, 2)[:, None, :, :]
    if gain is not None:
        product = product * gain
    return product.reshape(layers, outs, 5 * channels).astype(BF16)


def per_device(
    shot_feats,
    norm_gain,
    shot_taps,
    shot_mix,
    shot_bias,
    recv_taps,
    recv_mix,
    recv_bias,
    pack_index,
    recv_index,
):
    channels, shots_here, here, samples = shot_feats.shape
    blocks, capacity = pack_index.shape
    rows_here, fold = recv_index.shape
    slots = blocks * capacity

    tiles_all = lax.axis_size("recv")
    tile = lax.axis_index("recv")
    forward = [(i, i + 1) for i in range(tiles_all - 1)]
    backward = [(i + 1, i) for i in range(tiles_all - 1)]
    energy = lax.psum(jnp.sum(jnp.square(shot_feats.astype(F32)), axis=(0, 2, 3)), "recv")
    energy, upper, lower = lax.optimization_barrier(
        (energy, shot_feats[:, :, here - HALO :, :], shot_feats[:, :, :HALO, :])
    )
    low = lax.ppermute(upper, "recv", forward)
    high = lax.ppermute(lower, "recv", backward)
    inverse_rms = 1.0 / jnp.sqrt(energy / (channels * TRACES * samples) + 1e-05)

    packs = pack_index.reshape(-1)
    trace_id = jnp.arange(shots_here * here, dtype=jnp.int32)
    slot_id = jnp.arange(slots, dtype=jnp.int32)
    slot_of = jnp.sum(
        jnp.where(packs[None, :] == trace_id[:, None], slot_id[None, :], 0), axis=1
    ).astype(jnp.int32)

    send = slot_of
    edges = jnp.stack([tile == 0, tile == tiles_all - 1]).astype(jnp.int32)

    gain_rows = jnp.stack([norm_gain] + [jnp.ones_like(norm_gain)] * (LAYERS - 1))
    weights = mix_tables(shot_mix, shot_taps, gain_rows[:, None, None, :])
    bias = jnp.broadcast_to(shot_bias[:, :, None], shot_bias.shape + (samples,))
    taps = tap_tables(shot_taps)
    smem = pl.BlockSpec(memory_space=pltpu.SMEM)
    anywhere = pl.BlockSpec(memory_space=pl.ANY)
    packed_type = jax.ShapeDtypeStruct((slots, channels, LANES), BF16)
    table_specs = [
        whole(LAYERS, 5, channels, LANES),
        whole(LAYERS, channels, 5 * channels),
        whole(LAYERS, channels, samples),
    ]
    params = pltpu.CompilerParams(vmem_limit_bytes=48 * 2**20)
    tiles = samples // LANES
    inner_rows = here - 8
    main_spec = pl.BlockSpec((channels, 1, here, samples), lambda s: (0, s, 0, 0))
    halo_spec = pl.BlockSpec((channels, 1, HALO, samples), lambda s: (0, s, 0, 0))
    middle_spec = pl.BlockSpec((1, inner_rows, channels, samples), lambda s: (s, 0, 0, 0))
    middle, *packed = pl.pallas_call(
        inner_kernel,
        grid=(shots_here,),
        in_specs=[smem, smem, main_spec] + table_specs,
        out_specs=[middle_spec] + [anywhere] * CHUNKS,
        out_shape=[jax.ShapeDtypeStruct((shots_here, inner_rows, channels, samples), BF16)]
        + [packed_type] * CHUNKS,
        scratch_shapes=[
            pltpu.VMEM((tiles, channels * PITCH, LANES), F32),
            pltpu.VMEM((here, channels, samples), BF16),
            pltpu.VMEM((2, CHUNKS, here - 16, channels, LANES), BF16),
            pltpu.SemaphoreType.DMA((2,)),
        ],
        compiler_params=params,
        cost_estimate=pl.CostEstimate(
            flops=30 * 10**9, bytes_accessed=60 * 10**6, transcendentals=0
        ),
        name="shot_inner",
    )(inverse_rms, send, shot_feats, taps, weights, bias)
    packed = pl.pallas_call(
        edge_kernel,
        grid=(shots_here,),
        in_specs=[smem, smem, smem, main_spec, halo_spec, halo_spec, middle_spec]
        + table_specs
        + [anywhere] * CHUNKS,
        out_specs=[anywhere] * CHUNKS,
        out_shape=[packed_type] * CHUNKS,
        input_output_aliases={10 + i: i for i in range(CHUNKS)},
        scratch_shapes=[
            pltpu.VMEM((tiles, channels * PITCH, LANES), F32),
            pltpu.VMEM((4 * HALO, channels, samples), BF16),
            pltpu.VMEM((2, 16, channels, samples), BF16),
            pltpu.VMEM((2, CHUNKS, 16, channels, LANES), BF16),
            pltpu.SemaphoreType.DMA((2,)),
        ],
        compiler_params=params,
        name="shot_edges",
    )(inverse_rms, send, edges, shot_feats, low, high, middle, taps, weights, bias, *packed)

    buffers = [
        lax.all_to_all(
            part.reshape(blocks, capacity, channels, LANES),
            "shot",
            split_axis=0,
            concat_axis=0,
            tiled=True,
        ).reshape(slots, channels, LANES)
        for part in packed
    ]

    keep = jnp.maximum(recv_index.reshape(-1), 0)
    live_count = jnp.sum(recv_index >= 0, axis=1).astype(jnp.int32)
    recv_bias_rows = jnp.broadcast_to(recv_bias[:, :, None], recv_bias.shape + (samples,))
    return pl.pallas_call(
        recv_kernel,
        grid=(rows_here,),
        in_specs=[smem, smem] + table_specs + [anywhere] * CHUNKS,
        out_specs=pl.BlockSpec((channels, 1, fold, samples), lambda r: (0, r, 0, 0)),
        out_shape=jax.ShapeDtypeStruct((channels, rows_here, fold, samples), BF16),
        scratch_shapes=[
            pltpu.VMEM((2, CHUNKS, fold + 8, channels, LANES), BF16),
            pltpu.VMEM((fold + 8, channels, samples), BF16),
            pltpu.VMEM((tiles, channels * FOLDP, LANES), F32),
            pltpu.SemaphoreType.DMA((2,)),
        ],
        compiler_params=params,
        name="recv_domain",
    )(
        keep,
        live_count,
        tap_tables(recv_taps),
        mix_tables(recv_mix, recv_taps, None),
        recv_bias_rows,
        *buffers,
    )


def solution(mesh):
    return jax.shard_map(
        per_device,
        mesh=mesh,
        in_specs=(
            P(None, "shot", "recv", None),
            P(),
            P(),
            P(),
            P(),
            P(),
            P(),
            P(),
            P(("shot", "recv"), None),
            P(("shot", "recv"), None),
        ),
        out_specs=P(None, ("shot", "recv"), None, None),
        check_vma=False,
    )
```

```python
import functools

import jax
import jax.numpy as jnp
from jax import lax
from jax.experimental import pallas as pl
from jax.experimental.pallas import tpu as pltpu
from jax.sharding import PartitionSpec as P

TRACES = 256
LAYERS = 2
HALO = 8
GROUP = 8
CHUNKS = 3
PITCH = 33
FOLDP = 25
LANES = 128
BF16 = jnp.bfloat16
F32 = jnp.float32


def lagged(values, lag):
    if lag == 0:
        return values
    samples = values.shape[1]
    turned = pltpu.roll(values, (-lag) % samples, 1)
    lane = lax.broadcasted_iota(jnp.int32, values.shape, 1)
    inside = lane < samples - lag if lag > 0 else lane >= -lag
    return jnp.where(inside, turned, jnp.zeros((), values.dtype))


def group_linear(source, first, taps, weight, count):
    split = len(source.shape) == 4
    channels = source.shape[-2]
    part = 16
    tiles = source.shape[0] if split else source.shape[2] // LANES
    filtered = [[[None] * tiles for _ in range(channels // part)] for _ in range(count)]
    for h in range(channels // part):
        rows_at = slice(h * part, (h + 1) * part)
        for j in range(tiles):
            lanes_at = slice(j * LANES, (j + 1) * LANES)
            tap = [taps[k, rows_at, :] for k in range(5)]
            rows = [
                (
                    source[j, first + i, rows_at, :]
                    if split
                    else source[first + i, rows_at, lanes_at]
                ).astype(F32)
                for i in range(count + 8)
            ]
            for q in range(count):
                term = [rows[q + 2 * k] * tap[k] for k in range(5)]
                total = ((term[0] + term[1]) + (term[2] + term[3])) + term[4]
                filtered[q][h][j] = total.astype(BF16)
    outs = []
    for q in range(count):
        across = jnp.concatenate(
            [jnp.concatenate(pieces, axis=1) for pieces in filtered[q]], axis=0
        )
        stacked = jnp.concatenate([lagged(across, 2 * k - 4) for k in range(5)], axis=0)
        outs.append(jnp.dot(weight[...], stacked, preferred_element_type=F32))
    return outs


def last_layer(source, first, trace, base, send, packed, tables, staged, half, sems, at):
    taps, weights, bias = tables
    outs = group_linear(source, first, taps.at[1], weights.at[1], GROUP)
    for q in range(GROUP):
        value = jnp.maximum(outs[q] + bias[1], 0.0).astype(BF16)
        for j in range(CHUNKS):
            staged[half, j, at + q] = value[:, j * LANES : (j + 1) * LANES]
    for q in range(GROUP):
        slot = send[base + trace + q]
        for j in range(CHUNKS):
            pltpu.make_async_copy(
                staged.at[half, j, at + q], packed[j].at[slot], sems.at[half]
            ).start()


def drain(staged, packed, sems, half):
    for j in range(CHUNKS):
        pltpu.make_async_copy(
            staged.at[half, j], packed[j].at[pl.ds(0, staged.shape[2])], sems.at[half]
        ).wait()


def regroup(turned, grid_in, channels):
    span = grid_in.shape[0]

    def gather_trace(i, _):
        for q in range(8):
            t = i * 8 + q
            for j in range(turned.shape[0]):
                at = slice(j * LANES, (j + 1) * LANES)
                grid_in[t, :, at] = turned[j, pl.ds(t, channels, stride=PITCH), :].astype(BF16)
        return 0

    lax.fori_loop(0, span // 8, gather_trace, 0)


def inner_kernel(inverse_rms, send, main, taps, weights, bias, middle, *rest):
    packed, (turned, grid_in, staged, sems) = rest[:CHUNKS], rest[CHUNKS:]
    shot = pl.program_id(0)
    channels, _, here, samples = main.shape
    half = lax.rem(shot, 2)

    def load_channel(i, _):
        for q in range(4):
            c = i * 4 + q
            base = c * PITCH
            for j in range(turned.shape[0]):
                at = slice(j * LANES, (j + 1) * LANES)
                turned[j, pl.ds(base, here), :] = main[c, 0, :, at].astype(F32)
        return 0

    lax.fori_loop(0, channels // 4, load_channel, 0)
    regroup(turned, grid_in, channels)
    scale = inverse_rms[shot]

    def first_layer(i, _):
        outs = group_linear(grid_in, i * GROUP, taps.at[0], weights.at[0], GROUP)
        for q in range(GROUP):
            value = jnp.maximum(outs[q] * scale + bias[0], 0.0)
            middle[0, i * GROUP + q] = value.astype(BF16)
        return 0

    lax.fori_loop(0, (here - 8) // GROUP, first_layer, 0)

    @pl.when(shot >= 2)
    def _():
        drain(staged, packed, sems, half)

    def second_layer(i, _):
        last_layer(
            middle.at[0],
            i * GROUP,
            8 + i * GROUP,
            shot * here,
            send,
            packed,
            (taps, weights, bias),
            staged,
            half,
            sems,
            i * GROUP,
        )
        return 0

    lax.fori_loop(0, (here - 16) // GROUP, second_layer, 0)

    @pl.when(shot == pl.num_programs(0) - 1)
    def _():
        drain(staged, packed, sems, 1 - half)
        drain(staged, packed, sems, half)


def edge_kernel(inverse_rms, send, edges, main, low, high, middle, taps, weights, bias, *rest):
    rest = rest[CHUNKS:]
    packed, (turned, grid_in, joined, staged, sems) = rest[:CHUNKS], rest[CHUNKS:]
    shot = pl.program_id(0)
    channels, _, here, samples = main.shape
    span = 4 * HALO
    half = lax.rem(shot, 2)

    def load_channel(i, _):
        for q in range(4):
            c = i * 4 + q
            base = c * PITCH
            for j in range(turned.shape[0]):
                at = slice(j * LANES, (j + 1) * LANES)
                turned[j, pl.ds(base, HALO), :] = low[c, 0, :, at].astype(F32)
                turned[j, pl.ds(base + HALO, HALO), :] = main[c, 0, 0:16, at].astype(F32)[:HALO]
                turned[j, pl.ds(base + 2 * HALO, HALO), :] = main[
                    c, 0, here - 16 : here, at
                ].astype(F32)[16 - HALO :]
                turned[j, pl.ds(base + 3 * HALO, HALO), :] = high[c, 0, :, at].astype(F32)
        return 0

    lax.fori_loop(0, channels // 4, load_channel, 0)
    regroup(turned, grid_in, channels)
    scale = inverse_rms[shot]

    @pl.when(shot >= 2)
    def _():
        drain(staged, packed, sems, half)

    def one_side(side, _):
        outs = group_linear(grid_in, side * 16, taps.at[0], weights.at[0], GROUP)
        for q in range(GROUP):
            value = jnp.maximum(outs[q] * scale + bias[0], 0.0)
            joined[side, side * 8 + q] = value.astype(BF16)
            joined[side, 8 - side * 8 + q] = middle[0, side * 16 + q]

        @pl.when(edges[side] == 1)
        def _():
            joined[side, pl.ds(side * 12, 4)] = jnp.zeros((4, channels, samples), BF16)

        last_layer(
            joined.at[side],
            0,
            side * (here - 8),
            shot * here,
            send,
            packed,
            (taps, weights, bias),
            staged,
            half,
            sems,
            side * GROUP,
        )
        return 0

    lax.fori_loop(0, 2, one_side, 0)

    @pl.when(shot == pl.num_programs(0) - 1)
    def _():
        drain(staged, packed, sems, 1 - half)
        drain(staged, packed, sems, half)


def recv_kernel(first_call, keep, live_count, taps, weights, bias, *rest):
    buffers, rest = rest[:2], rest[2:]
    if first_call:
        out, seam = rest[:2]
    else:
        seam, out = rest[0], rest[2]
    gathered, middle, turned, sems = rest[-4:]
    row = pl.program_id(0)
    rows = pl.num_programs(0)
    channels, _, fold, _ = out.shape
    tiles = len(buffers)
    samples = tiles * LANES
    half = lax.rem(row, 2)

    def fetch(r, into):
        def one(i, _):
            for q in range(4):
                k = i * 4 + q
                slot = keep[r * fold + k]
                for j in range(tiles):
                    pltpu.make_async_copy(
                        buffers[j].at[slot], gathered.at[into, j, 4 + k], sems.at[into]
                    ).start()
            return 0

        lax.fori_loop(0, fold // 4, one, 0)

    @pl.when(row == 0)
    def _():
        fetch(0, 0)
        edge = jnp.zeros((4, channels, samples), BF16)
        for which in range(2):
            for j in range(tiles):
                gathered[which, j, 0:4] = edge[:, :, :LANES]
                gathered[which, j, fold + 4 : fold + 8] = edge[:, :, :LANES]
        middle[0:4] = edge
        middle[fold + 4 : fold + 8] = edge

    @pl.when(row + 1 < rows)
    def _():
        fetch(row + 1, 1 - half)

    for j in range(tiles):
        pltpu.make_async_copy(
            buffers[j].at[pl.ds(0, fold)], gathered.at[half, j, pl.ds(4, fold)], sems.at[half]
        ).wait()
    live = live_count[row]

    def clear(k, _):
        for j in range(tiles):
            gathered[half, j, 4 + k] = jnp.zeros((channels, LANES), BF16)
        return 0

    lax.fori_loop(live, fold, clear, 0)
    groups = (live + GROUP - 1) // GROUP

    def first_layer(i, _):
        outs = group_linear(gathered.at[half], i * GROUP, taps.at[0], weights.at[0], GROUP)
        for q in range(GROUP):
            k = i * GROUP + q
            value = jnp.maximum(outs[q] + bias[0, :, :samples], 0.0)
            middle[4 + k] = jnp.where(k < live, value, 0.0).astype(BF16)
        return 0

    lax.fori_loop(0, groups, first_layer, 0)

    def clear_rest(k, _):
        middle[4 + k] = jnp.zeros((channels, samples), BF16)
        for j in range(tiles):
            turned[j, pl.ds(k, channels, stride=FOLDP), :] = jnp.zeros((channels, LANES), F32)
        return 0

    lax.fori_loop(groups * GROUP, fold, clear_rest, 0)

    def second_layer(i, _):
        outs = group_linear(middle, i * GROUP, taps.at[1], weights.at[1], GROUP)
        for q in range(GROUP):
            k = i * GROUP + q
            value = jnp.where(k < live, jnp.maximum(outs[q] + bias[1, :, :samples], 0.0), 0.0)
            for j in range(tiles):
                turned[j, pl.ds(k, channels, stride=FOLDP), :] = value[:, j * LANES : (j + 1) * LANES]
        return 0

    lax.fori_loop(0, groups, second_layer, 0)

    near = lax.broadcasted_iota(jnp.int32, (fold, LANES), 1) < LANES // 2

    def store_channel(i, _):
        for q in range(4):
            c = i * 4 + q
            base = c * FOLDP
            left = turned[0, pl.ds(base, fold), :]
            right = turned[1, pl.ds(base, fold), :]
            if first_call:
                seam[c, 0] = left.astype(BF16)
                out[c, 0] = right.astype(BF16)
            else:
                out[c, 0, :, :LANES] = left.astype(BF16)
                joined = jnp.where(near, right, seam[c, 0].astype(F32))
                out[c, 0, :, LANES:] = joined.astype(BF16)
        return 0

    lax.fori_loop(0, channels // 4, store_channel, 0)


def whole(*shape):
    return pl.BlockSpec(shape, lambda *_: (0,) * len(shape))


def tap_tables(taps):
    table = jnp.swapaxes(taps[:, 0], 1, 2)[..., None]
    return jnp.broadcast_to(table, table.shape[:-1] + (LANES,)).astype(F32)


def mix_tables(mix, taps, gain):
    layers, outs, channels = mix.shape
    product = mix.astype(F32)[:, :, None, :] * jnp.swapaxes(taps[:, 1], 1, 2)[:, None, :, :]
    if gain is not None:
        product = product * gain
    return product.reshape(layers, outs, 5 * channels).astype(BF16)


def per_device(
    shot_feats,
    norm_gain,
    shot_taps,
    shot_mix,
    shot_bias,
    recv_taps,
    recv_mix,
    recv_bias,
    pack_index,
    recv_index,
):
    channels, shots_here, here, samples = shot_feats.shape
    blocks, capacity = pack_index.shape
    rows_here, fold = recv_index.shape
    slots = blocks * capacity

    tiles_all = lax.axis_size("recv")
    tile = lax.axis_index("recv")
    forward = [(i, i + 1) for i in range(tiles_all - 1)]
    backward = [(i + 1, i) for i in range(tiles_all - 1)]
    energy = lax.psum(jnp.sum(jnp.square(shot_feats.astype(F32)), axis=(0, 2, 3)), "recv")
    energy, upper, lower = lax.optimization_barrier(
        (energy, shot_feats[:, :, here - HALO :, :], shot_feats[:, :, :HALO, :])
    )
    low = lax.ppermute(upper, "recv", forward)
    high = lax.ppermute(lower, "recv", backward)
    inverse_rms = 1.0 / jnp.sqrt(energy / (channels * TRACES * samples) + 1e-05)

    packs = pack_index.reshape(-1)
    trace_id = jnp.arange(shots_here * here, dtype=jnp.int32)
    slot_id = jnp.arange(slots, dtype=jnp.int32)
    slot_of = jnp.sum(
        jnp.where(packs[None, :] == trace_id[:, None], slot_id[None, :], 0), axis=1
    ).astype(jnp.int32)

    send = slot_of
    edges = jnp.stack([tile == 0, tile == tiles_all - 1]).astype(jnp.int32)

    gain_rows = jnp.stack([norm_gain] + [jnp.ones_like(norm_gain)] * (LAYERS - 1))
    weights = mix_tables(shot_mix, shot_taps, gain_rows[:, None, None, :])
    bias = jnp.broadcast_to(shot_bias[:, :, None], shot_bias.shape + (samples,))
    taps = tap_tables(shot_taps)
    smem = pl.BlockSpec(memory_space=pltpu.SMEM)
    anywhere = pl.BlockSpec(memory_space=pl.ANY)
    packed_type = jax.ShapeDtypeStruct((slots, channels, LANES), BF16)
    table_specs = [
        whole(LAYERS, 5, channels, LANES),
        whole(LAYERS, channels, 5 * channels),
        whole(LAYERS, channels, samples),
    ]
    params = pltpu.CompilerParams(vmem_limit_bytes=48 * 2**20)
    tiles = samples // LANES
    inner_rows = here - 8
    main_spec = pl.BlockSpec((channels, 1, here, samples), lambda s: (0, s, 0, 0))
    halo_spec = pl.BlockSpec((channels, 1, HALO, samples), lambda s: (0, s, 0, 0))
    middle_spec = pl.BlockSpec((1, inner_rows, channels, samples), lambda s: (s, 0, 0, 0))
    middle, *packed = pl.pallas_call(
        inner_kernel,
        grid=(shots_here,),
        in_specs=[smem, smem, main_spec] + table_specs,
        out_specs=[middle_spec] + [anywhere] * CHUNKS,
        out_shape=[jax.ShapeDtypeStruct((shots_here, inner_rows, channels, samples), BF16)]
        + [packed_type] * CHUNKS,
        scratch_shapes=[
            pltpu.VMEM((tiles, channels * PITCH, LANES), F32),
            pltpu.VMEM((here, channels, samples), BF16),
            pltpu.VMEM((2, CHUNKS, here - 16, channels, LANES), BF16),
            pltpu.SemaphoreType.DMA((2,)),
        ],
        compiler_params=params,
        cost_estimate=pl.CostEstimate(
            flops=30 * 10**9, bytes_accessed=60 * 10**6, transcendentals=0
        ),
        name="shot_inner",
    )(inverse_rms, send, shot_feats, taps, weights, bias)
    packed = pl.pallas_call(
        edge_kernel,
        grid=(shots_here,),
        in_specs=[smem, smem, smem, main_spec, halo_spec, halo_spec, middle_spec]
        + table_specs
        + [anywhere] * CHUNKS,
        out_specs=[anywhere] * CHUNKS,
        out_shape=[packed_type] * CHUNKS,
        input_output_aliases={10 + i: i for i in range(CHUNKS)},
        scratch_shapes=[
            pltpu.VMEM((tiles, channels * PITCH, LANES), F32),
            pltpu.VMEM((4 * HALO, channels, samples), BF16),
            pltpu.VMEM((2, 16, channels, samples), BF16),
            pltpu.VMEM((2, CHUNKS, 16, channels, LANES), BF16),
            pltpu.SemaphoreType.DMA((2,)),
        ],
        compiler_params=params,
        name="shot_edges",
    )(inverse_rms, send, edges, shot_feats, low, high, middle, taps, weights, bias, *packed)

    def exchange(part):
        return lax.all_to_all(
            part.reshape(blocks, capacity, channels, LANES),
            "shot",
            split_axis=0,
            concat_axis=0,
            tiled=True,
        ).reshape(slots, channels, LANES)

    third = exchange(packed[2])
    second = exchange(packed[1])
    second, third, waiting = lax.optimization_barrier((second, third, packed[0]))
    first = exchange(waiting)

    keep = jnp.maximum(recv_index.reshape(-1), 0)
    live_count = jnp.sum(recv_index >= 0, axis=1).astype(jnp.int32)
    tables = (
        keep,
        live_count,
        tap_tables(recv_taps),
        mix_tables(recv_mix, recv_taps, None),
        jnp.broadcast_to(recv_bias[:, :, None], recv_bias.shape + (samples,)),
    )
    out_type = jax.ShapeDtypeStruct((channels, rows_here, fold, samples), BF16)
    seam_type = jax.ShapeDtypeStruct((channels, rows_here, fold, LANES), BF16)

    def lanes_spec(width, at):
        return pl.BlockSpec((channels, 1, fold, width), lambda r: (0, r, 0, at))

    scratch = [
        pltpu.VMEM((2, 2, fold + 8, channels, LANES), BF16),
        pltpu.VMEM((fold + 8, channels, 2 * LANES), BF16),
        pltpu.VMEM((2, channels * FOLDP, LANES), F32),
        pltpu.SemaphoreType.DMA((2,)),
    ]
    base_specs = [smem, smem] + table_specs + [anywhere] * 2
    out, seam = pl.pallas_call(
        functools.partial(recv_kernel, True),
        grid=(rows_here,),
        in_specs=base_specs,
        out_specs=[lanes_spec(LANES, 2), lanes_spec(LANES, 0)],
        out_shape=[out_type, seam_type],
        scratch_shapes=scratch,
        compiler_params=params,
        cost_estimate=pl.CostEstimate(
            flops=30 * 10**9, bytes_accessed=60 * 10**6, transcendentals=0
        ),
        name="recv_right",
    )(*tables, second, third)
    return pl.pallas_call(
        functools.partial(recv_kernel, False),
        grid=(rows_here,),
        in_specs=base_specs + [lanes_spec(LANES, 0), anywhere],
        out_specs=lanes_spec(2 * LANES, 0),
        out_shape=out_type,
        input_output_aliases={8: 0},
        scratch_shapes=scratch,
        compiler_params=params,
        name="recv_left",
    )(*tables, first, second, seam, out)


def solution(mesh):
    return jax.shard_map(
        per_device,
        mesh=mesh,
        in_specs=(
            P(None, "shot", "recv", None),
            P(),
            P(),
            P(),
            P(),
            P(),
            P(),
            P(),
            P(("shot", "recv"), None),
            P(("shot", "recv"), None),
        ),
        out_specs=P(None, ("shot", "recv"), None, None),
        check_vma=False,
    )
```

```python
import jax
import jax.numpy as jnp
from jax import lax
from jax.experimental import pallas as pl
from jax.experimental.pallas import tpu as pltpu
from jax.sharding import PartitionSpec as P

TRACES = 256
LAYERS = 2
HALO = 8
GROUP = 8
CHUNKS = 3
PITCH = 33
FOLDP = 25
LANES = 128
BF16 = jnp.bfloat16
F32 = jnp.float32


def lagged(values, lag):
    if lag == 0:
        return values
    samples = values.shape[1]
    turned = pltpu.roll(values, (-lag) % samples, 1)
    lane = lax.broadcasted_iota(jnp.int32, values.shape, 1)
    inside = lane < samples - lag if lag > 0 else lane >= -lag
    return jnp.where(inside, turned, jnp.zeros((), values.dtype))


def group_linear(source, first, taps, weight, count):
    split = len(source.shape) == 4
    channels = source.shape[-2]
    part = 16
    tiles = source.shape[0] if split else source.shape[2] // LANES
    filtered = [[[None] * tiles for _ in range(channels // part)] for _ in range(count)]
    for h in range(channels // part):
        rows_at = slice(h * part, (h + 1) * part)
        for j in range(tiles):
            lanes_at = slice(j * LANES, (j + 1) * LANES)
            tap = [taps[k, rows_at, :] for k in range(5)]
            rows = [
                (
                    source[j, first + i, rows_at, :]
                    if split
                    else source[first + i, rows_at, lanes_at]
                ).astype(F32)
                for i in range(count + 8)
            ]
            for q in range(count):
                term = [rows[q + 2 * k] * tap[k] for k in range(5)]
                total = ((term[0] + term[1]) + (term[2] + term[3])) + term[4]
                filtered[q][h][j] = total.astype(BF16)
    outs = []
    for q in range(count):
        across = jnp.concatenate(
            [jnp.concatenate(pieces, axis=1) for pieces in filtered[q]], axis=0
        )
        stacked = jnp.concatenate([lagged(across, 2 * k - 4) for k in range(5)], axis=0)
        outs.append(jnp.dot(weight[...], stacked, preferred_element_type=F32))
    return outs


def last_layer(source, first, trace, base, send, packed, tables, staged, half, sems, at):
    taps, weights, bias = tables
    outs = group_linear(source, first, taps.at[1], weights.at[1], GROUP)
    for q in range(GROUP):
        value = jnp.maximum(outs[q] + bias[1], 0.0).astype(BF16)
        for j in range(CHUNKS):
            staged[half, j, at + q] = value[:, j * LANES : (j + 1) * LANES]
    for q in range(GROUP):
        slot = send[base + trace + q]
        for j in range(CHUNKS):
            pltpu.make_async_copy(
                staged.at[half, j, at + q], packed[j].at[slot], sems.at[half]
            ).start()


def drain(staged, packed, sems, half):
    for j in range(CHUNKS):
        pltpu.make_async_copy(
            staged.at[half, j], packed[j].at[pl.ds(0, staged.shape[2])], sems.at[half]
        ).wait()


def regroup(turned, grid_in, channels):
    span = grid_in.shape[0]

    def gather_trace(i, _):
        for q in range(8):
            t = i * 8 + q
            for j in range(turned.shape[0]):
                at = slice(j * LANES, (j + 1) * LANES)
                grid_in[t, :, at] = turned[j, pl.ds(t, channels, stride=PITCH), :].astype(BF16)
        return 0

    lax.fori_loop(0, span // 8, gather_trace, 0)


def inner_kernel(inverse_rms, send, main, taps, weights, bias, middle, *rest):
    packed, (turned, grid_in, staged, sems) = rest[:CHUNKS], rest[CHUNKS:]
    shot = pl.program_id(0)
    channels, _, here, samples = main.shape
    half = lax.rem(shot, 2)

    def load_channel(i, _):
        for q in range(4):
            c = i * 4 + q
            base = c * PITCH
            for j in range(turned.shape[0]):
                at = slice(j * LANES, (j + 1) * LANES)
                turned[j, pl.ds(base, here), :] = main[c, 0, :, at].astype(F32)
        return 0

    lax.fori_loop(0, channels // 4, load_channel, 0)
    regroup(turned, grid_in, channels)
    scale = inverse_rms[shot]

    def first_layer(i, _):
        outs = group_linear(grid_in, i * GROUP, taps.at[0], weights.at[0], GROUP)
        for q in range(GROUP):
            value = jnp.maximum(outs[q] * scale + bias[0], 0.0)
            middle[0, i * GROUP + q] = value.astype(BF16)
        return 0

    lax.fori_loop(0, (here - 8) // GROUP, first_layer, 0)

    @pl.when(shot >= 2)
    def _():
        drain(staged, packed, sems, half)

    def second_layer(i, _):
        last_layer(
            middle.at[0],
            i * GROUP,
            8 + i * GROUP,
            shot * here,
            send,
            packed,
            (taps, weights, bias),
            staged,
            half,
            sems,
            i * GROUP,
        )
        return 0

    lax.fori_loop(0, (here - 16) // GROUP, second_layer, 0)

    @pl.when(shot == pl.num_programs(0) - 1)
    def _():
        drain(staged, packed, sems, 1 - half)
        drain(staged, packed, sems, half)


def edge_kernel(inverse_rms, send, edges, main, low, high, middle, taps, weights, bias, *rest):
    rest = rest[CHUNKS:]
    packed, (turned, grid_in, joined, staged, sems) = rest[:CHUNKS], rest[CHUNKS:]
    shot = pl.program_id(0)
    channels, _, here, samples = main.shape
    span = 4 * HALO
    half = lax.rem(shot, 2)

    def load_channel(i, _):
        for q in range(4):
            c = i * 4 + q
            base = c * PITCH
            for j in range(turned.shape[0]):
                at = slice(j * LANES, (j + 1) * LANES)
                turned[j, pl.ds(base, HALO), :] = low[c, 0, :, at].astype(F32)
                turned[j, pl.ds(base + HALO, HALO), :] = main[c, 0, 0:16, at].astype(F32)[:HALO]
                turned[j, pl.ds(base + 2 * HALO, HALO), :] = main[
                    c, 0, here - 16 : here, at
                ].astype(F32)[16 - HALO :]
                turned[j, pl.ds(base + 3 * HALO, HALO), :] = high[c, 0, :, at].astype(F32)
        return 0

    lax.fori_loop(0, channels // 4, load_channel, 0)
    regroup(turned, grid_in, channels)
    scale = inverse_rms[shot]

    @pl.when(shot >= 2)
    def _():
        drain(staged, packed, sems, half)

    def one_side(side, _):
        outs = group_linear(grid_in, side * 16, taps.at[0], weights.at[0], GROUP)
        for q in range(GROUP):
            value = jnp.maximum(outs[q] * scale + bias[0], 0.0)
            joined[side, side * 8 + q] = value.astype(BF16)
            joined[side, 8 - side * 8 + q] = middle[0, side * 16 + q]

        @pl.when(edges[side] == 1)
        def _():
            joined[side, pl.ds(side * 12, 4)] = jnp.zeros((4, channels, samples), BF16)

        last_layer(
            joined.at[side],
            0,
            side * (here - 8),
            shot * here,
            send,
            packed,
            (taps, weights, bias),
            staged,
            half,
            sems,
            side * GROUP,
        )
        return 0

    lax.fori_loop(0, 2, one_side, 0)

    @pl.when(shot == pl.num_programs(0) - 1)
    def _():
        drain(staged, packed, sems, 1 - half)
        drain(staged, packed, sems, half)


def recv_kernel(
    keep,
    live_count,
    taps,
    weights,
    bias,
    *rest,
):
    buffers, (out, gathered, middle, turned, sems) = rest[:CHUNKS], rest[CHUNKS:]
    row = pl.program_id(0)
    rows = pl.num_programs(0)
    channels, _, fold, samples = out.shape
    tiles = samples // LANES
    half = lax.rem(row, 2)

    def fetch(r, into):
        def one(i, _):
            for q in range(4):
                k = i * 4 + q
                slot = keep[r * fold + k]
                for j in range(CHUNKS):
                    pltpu.make_async_copy(
                        buffers[j].at[slot], gathered.at[into, j, 4 + k], sems.at[into]
                    ).start()
            return 0

        lax.fori_loop(0, fold // 4, one, 0)

    @pl.when(row == 0)
    def _():
        fetch(0, 0)
        edge = jnp.zeros((4, channels, samples), BF16)
        for which in range(2):
            for j in range(CHUNKS):
                gathered[which, j, 0:4] = edge[:, :, :LANES]
                gathered[which, j, fold + 4 : fold + 8] = edge[:, :, :LANES]
        middle[0:4] = edge
        middle[fold + 4 : fold + 8] = edge

    @pl.when(row + 1 < rows)
    def _():
        fetch(row + 1, 1 - half)

    for j in range(CHUNKS):
        pltpu.make_async_copy(
            buffers[j].at[pl.ds(0, fold)], gathered.at[half, j, pl.ds(4, fold)], sems.at[half]
        ).wait()
    live = live_count[row]

    def clear(k, _):
        for j in range(CHUNKS):
            gathered[half, j, 4 + k] = jnp.zeros((channels, LANES), BF16)
        return 0

    lax.fori_loop(live, fold, clear, 0)
    groups = (live + GROUP - 1) // GROUP

    def first_layer(i, _):
        outs = group_linear(gathered.at[half], i * GROUP, taps.at[0], weights.at[0], GROUP)
        for q in range(GROUP):
            k = i * GROUP + q
            value = jnp.maximum(outs[q] + bias[0], 0.0)
            middle[4 + k] = jnp.where(k < live, value, 0.0).astype(BF16)
        return 0

    lax.fori_loop(0, groups, first_layer, 0)

    def clear_rest(k, _):
        middle[4 + k] = jnp.zeros((channels, samples), BF16)
        for j in range(tiles):
            turned[j, pl.ds(k, channels, stride=FOLDP), :] = jnp.zeros((channels, LANES), F32)
        return 0

    lax.fori_loop(groups * GROUP, fold, clear_rest, 0)

    def second_layer(i, _):
        outs = group_linear(middle, i * GROUP, taps.at[1], weights.at[1], GROUP)
        for q in range(GROUP):
            k = i * GROUP + q
            value = jnp.where(k < live, jnp.maximum(outs[q] + bias[1], 0.0), 0.0)
            for j in range(tiles):
                turned[j, pl.ds(k, channels, stride=FOLDP), :] = value[:, j * LANES : (j + 1) * LANES]
        return 0

    lax.fori_loop(0, groups, second_layer, 0)

    def store_channel(i, _):
        for q in range(4):
            c = i * 4 + q
            base = c * FOLDP
            for j in range(tiles):
                out[c, 0, :, j * LANES : (j + 1) * LANES] = turned[j, pl.ds(base, fold), :].astype(BF16)
        return 0

    lax.fori_loop(0, channels // 4, store_channel, 0)


def whole(*shape):
    return pl.BlockSpec(shape, lambda *_: (0,) * len(shape))


def tap_tables(taps):
    table = jnp.swapaxes(taps[:, 0], 1, 2)[..., None]
    return jnp.broadcast_to(table, table.shape[:-1] + (LANES,)).astype(F32)


def mix_tables(mix, taps, gain):
    layers, outs, channels = mix.shape
    product = mix.astype(F32)[:, :, None, :] * jnp.swapaxes(taps[:, 1], 1, 2)[:, None, :, :]
    if gain is not None:
        product = product * gain
    return product.reshape(layers, outs, 5 * channels).astype(BF16)


def per_device(
    shot_feats,
    norm_gain,
    shot_taps,
    shot_mix,
    shot_bias,
    recv_taps,
    recv_mix,
    recv_bias,
    pack_index,
    recv_index,
):
    channels, shots_here, here, samples = shot_feats.shape
    blocks, capacity = pack_index.shape
    rows_here, fold = recv_index.shape
    slots = blocks * capacity

    tiles_all = lax.axis_size("recv")
    tile = lax.axis_index("recv")
    forward = [(i, i + 1) for i in range(tiles_all - 1)]
    backward = [(i + 1, i) for i in range(tiles_all - 1)]
    energy = lax.psum(jnp.sum(jnp.square(shot_feats.astype(F32)), axis=(0, 2, 3)), "recv")
    energy, upper, lower = lax.optimization_barrier(
        (energy, shot_feats[:, :, here - HALO :, :], shot_feats[:, :, :HALO, :])
    )
    low = lax.ppermute(upper, "recv", forward)
    high = lax.ppermute(lower, "recv", backward)
    inverse_rms = 1.0 / jnp.sqrt(energy / (channels * TRACES * samples) + 1e-05)

    packs = pack_index.reshape(-1)
    trace_id = jnp.arange(shots_here * here, dtype=jnp.int32)
    slot_id = jnp.arange(slots, dtype=jnp.int32)
    slot_of = jnp.sum(
        jnp.where(packs[None, :] == trace_id[:, None], slot_id[None, :], 0), axis=1
    ).astype(jnp.int32)

    send = slot_of
    edges = jnp.stack([tile == 0, tile == tiles_all - 1]).astype(jnp.int32)

    gain_rows = jnp.stack([norm_gain] + [jnp.ones_like(norm_gain)] * (LAYERS - 1))
    weights = mix_tables(shot_mix, shot_taps, gain_rows[:, None, None, :])
    bias = jnp.broadcast_to(shot_bias[:, :, None], shot_bias.shape + (samples,))
    taps = tap_tables(shot_taps)
    smem = pl.BlockSpec(memory_space=pltpu.SMEM)
    anywhere = pl.BlockSpec(memory_space=pl.ANY)
    packed_type = jax.ShapeDtypeStruct((slots, channels, LANES), BF16)
    table_specs = [
        whole(LAYERS, 5, channels, LANES),
        whole(LAYERS, channels, 5 * channels),
        whole(LAYERS, channels, samples),
    ]
    params = pltpu.CompilerParams(vmem_limit_bytes=58 * 2**20)
    tiles = samples // LANES
    inner_rows = here - 8
    main_spec = pl.BlockSpec((channels, 1, here, samples), lambda s: (0, s, 0, 0))
    halo_spec = pl.BlockSpec((channels, 1, HALO, samples), lambda s: (0, s, 0, 0))
    middle_spec = pl.BlockSpec((1, inner_rows, channels, samples), lambda s: (s, 0, 0, 0))
    middle, *packed = pl.pallas_call(
        inner_kernel,
        grid=(shots_here,),
        in_specs=[smem, smem, main_spec] + table_specs,
        out_specs=[middle_spec] + [anywhere] * CHUNKS,
        out_shape=[jax.ShapeDtypeStruct((shots_here, inner_rows, channels, samples), BF16)]
        + [packed_type] * CHUNKS,
        scratch_shapes=[
            pltpu.VMEM((tiles, channels * PITCH, LANES), F32),
            pltpu.VMEM((here, channels, samples), BF16),
            pltpu.VMEM((2, CHUNKS, here - 16, channels, LANES), BF16),
            pltpu.SemaphoreType.DMA((2,)),
        ],
        compiler_params=params,
        cost_estimate=pl.CostEstimate(
            flops=30 * 10**9, bytes_accessed=60 * 10**6, transcendentals=0
        ),
        name="shot_inner",
    )(inverse_rms, send, shot_feats, taps, weights, bias)
    packed = pl.pallas_call(
        edge_kernel,
        grid=(shots_here,),
        in_specs=[smem, smem, smem, main_spec, halo_spec, halo_spec, middle_spec]
        + table_specs
        + [anywhere] * CHUNKS,
        out_specs=[anywhere] * CHUNKS,
        out_shape=[packed_type] * CHUNKS,
        input_output_aliases={10 + i: i for i in range(CHUNKS)},
        scratch_shapes=[
            pltpu.VMEM((tiles, channels * PITCH, LANES), F32),
            pltpu.VMEM((4 * HALO, channels, samples), BF16),
            pltpu.VMEM((2, 16, channels, samples), BF16),
            pltpu.VMEM((2, CHUNKS, 16, channels, LANES), BF16),
            pltpu.SemaphoreType.DMA((2,)),
        ],
        compiler_params=params,
        name="shot_edges",
    )(inverse_rms, send, edges, shot_feats, low, high, middle, taps, weights, bias, *packed)

    buffers = [
        lax.all_to_all(
            part.reshape(blocks, capacity, channels, LANES),
            "shot",
            split_axis=0,
            concat_axis=0,
            tiled=True,
        ).reshape(slots, channels, LANES)
        for part in packed
    ]

    keep = jnp.maximum(recv_index.reshape(-1), 0)
    live_count = jnp.sum(recv_index >= 0, axis=1).astype(jnp.int32)
    recv_bias_rows = jnp.broadcast_to(recv_bias[:, :, None], recv_bias.shape + (samples,))
    return pl.pallas_call(
        recv_kernel,
        grid=(rows_here,),
        in_specs=[smem, smem] + table_specs + [anywhere] * CHUNKS,
        out_specs=pl.BlockSpec((channels, 1, fold, samples), lambda r: (0, r, 0, 0)),
        out_shape=jax.ShapeDtypeStruct((channels, rows_here, fold, samples), BF16),
        scratch_shapes=[
            pltpu.VMEM((2, CHUNKS, fold + 8, channels, LANES), BF16),
            pltpu.VMEM((fold + 8, channels, samples), BF16),
            pltpu.VMEM((tiles, channels * FOLDP, LANES), F32),
            pltpu.SemaphoreType.DMA((2,)),
        ],
        compiler_params=params,
        name="recv_domain",
    )(
        keep,
        live_count,
        tap_tables(recv_taps),
        mix_tables(recv_mix, recv_taps, None),
        recv_bias_rows,
        *buffers,
    )


def solution(mesh):
    return jax.shard_map(
        per_device,
        mesh=mesh,
        in_specs=(
            P(None, "shot", "recv", None),
            P(),
            P(),
            P(),
            P(),
            P(),
            P(),
            P(),
            P(("shot", "recv"), None),
            P(("shot", "recv"), None),
        ),
        out_specs=P(None, ("shot", "recv"), None, None),
        check_vma=False,
    )
```
